32 devices in a mesh: dp: 8 (over z, y), tensor: 4 (over x, core).
Axes of the slice: x: 2, y: 2, z: 4, core: 2. Of those that a mesh axis runs over, the one named last changes fastest.
Arguments:
- grad_query: bfloat16 [8, 1, 4096, 4608], P('dp', None, 'tensor'), may hold values from -33 to 33
- grad_key: bfloat16 [8, 1, 2048, 4608], P('dp', None, 'tensor'), may hold values from -33 to 33
- error_query: bfloat16 [8, 1, 4096, 4608], P('dp', None, 'tensor'), may hold values from -12 to 12
- error_key: bfloat16 [8, 1, 2048, 4608], P('dp', None, 'tensor'), may hold values from -12 to 12
- factor_query: bfloat16 [1, 4608, 64], replicated, may hold values from -0.09375 to 0.09375
- factor_key: bfloat16 [1, 4608, 64], replicated, may hold values from -0.09375 to 0.09375
Outputs:
- error_query_new: bfloat16 [8, 1, 4096, 4608], P('dp', None, 'tensor')
- error_key_new: bfloat16 [8, 1, 2048, 4608], P('dp', None, 'tensor')
- factor_query_new: bfloat16 [1, 4608, 64], replicated
- factor_key_new: bfloat16 [1, 4608, 64], replicated
The draws below stay inside these ranges and needn't reach their ends.
All inputs are finite; a program needn't handle non-finite values.
Results may differ from the reference program's by a relative error of at most 0.0085.
Values may be sent and summed in bfloat16 or wider, within the bound.
No kernel may reach another device: no remote copies, remote signals or barrier semaphores. Data moves between devices by JAX's collectives and lax.ppermute only.
A program may use at most 128 MiB of HBM per device.

```python
import math
import jax
import jax.numpy as jnp
from jax import lax

D = 4608
HQ = 4096
HK = 2048
RANK = 64
LAYERS = 1
REPLICAS = 8
N_DP = 8


def row_col_scales(key, salt, rows, ramp):
    key = jax.random.fold_in(key, salt)
    key_rows, key_cols = jax.random.split(key)
    row_scale = jnp.exp(jax.random.uniform(key_rows, (rows,), jnp.float32, math.log(0.3), 0.0))
    position = jnp.arange(rows, dtype=jnp.float32) / (rows - 1)
    row_scale = row_scale * jnp.power(ramp, position)
    col_scale = jnp.exp(jax.random.uniform(key_cols, (D,), jnp.float32, math.log(0.15), math.log(1.5)))
    return (row_scale, col_scale)


def shaped(key, rows, ramp, salt, amplitude):
    row_scale, col_scale = row_col_scales(key, salt, rows, ramp)
    return row_scale[:, None] * col_scale[None, :] * amplitude


def draw_grad_query(key, part):
    ramp = 3.0
    scale = shaped(key, HQ, ramp, 11, 1.0)
    key = jax.random.fold_in(key, 1)
    noise = jnp.clip(jax.random.normal(key, (REPLICAS, LAYERS, HQ, D), jnp.float32), -4.0, 4.0)
    return (noise * scale).astype(jnp.bfloat16)


def draw_grad_key(key, part):
    ramp = 3.0
    scale = shaped(key, HK, ramp, 12, 1.0)
    key = jax.random.fold_in(key, 2)
    noise = jnp.clip(jax.random.normal(key, (REPLICAS, LAYERS, HK, D), jnp.float32), -4.0, 4.0)
    return (noise * scale).astype(jnp.bfloat16)


def draw_error_query(key, part):
    ramp = 3.0
    scale = shaped(key, HQ, ramp, 11, 0.5)
    key = jax.random.fold_in(key, 3)
    noise = jnp.clip(jax.random.normal(key, (REPLICAS, LAYERS, HQ, D), jnp.float32), -4.0, 4.0)
    return (noise * scale).astype(jnp.bfloat16)


def draw_error_key(key, part):
    ramp = 3.0
    scale = shaped(key, HK, ramp, 12, 0.5)
    key = jax.random.fold_in(key, 4)
    noise = jnp.clip(jax.random.normal(key, (REPLICAS, LAYERS, HK, D), jnp.float32), -4.0, 4.0)
    return (noise * scale).astype(jnp.bfloat16)


def scatter_about(key, dims, spread, most, kind=jnp.bfloat16):
    result = spread * jax.random.normal(key, dims, jnp.float32)
    return jnp.clip(result, min=-most, max=most).astype(kind)


def setup_inputs(seed: int = 0) -> dict:
    splits = jax.random.split(jax.random.key(seed), 7)
    grad_query = draw_grad_query(jax.random.fold_in(splits[6], 71), 0)
    grad_key = draw_grad_key(jax.random.fold_in(splits[6], 71), 0)
    error_query = draw_error_query(jax.random.fold_in(splits[6], 71), 0)
    error_key = draw_error_key(jax.random.fold_in(splits[6], 71), 0)
    factor_query = scatter_about(splits[4], (LAYERS, D, RANK), D ** -0.5, 0.09375)
    factor_key = scatter_about(splits[5], (LAYERS, D, RANK), D ** -0.5, 0.09375)
    return dict(grad_query=grad_query, grad_key=grad_key, error_query=error_query, error_key=error_key, factor_query=factor_query, factor_key=factor_key)


def merge(grad, error):
    return (grad.astype(jnp.float32) + error.astype(jnp.float32)).astype(jnp.bfloat16)

def compress(grads, errors, factor):
    factor_wide = factor.astype(jnp.float32)

    def add_image(total, pair):
        merged = merge(pair[0], pair[1]).astype(jnp.float32)
        return (total + jnp.einsum('lhd,ldr->lhr', merged, factor_wide, precision=lax.Precision.HIGHEST), None)
    start = jnp.zeros((grads.shape[1], grads.shape[2], factor.shape[2]), jnp.float32)
    image, _ = lax.scan(add_image, start, (grads, errors))
    gram = jnp.einsum('lhr,lhs->lrs', image, image, precision=lax.Precision.HIGHEST)
    lower = jnp.linalg.cholesky(gram)
    solved = jax.scipy.linalg.solve_triangular(lower, jnp.swapaxes(image, 1, 2), lower=True)
    basis = jnp.swapaxes(solved, 1, 2).astype(jnp.bfloat16)
    basis_wide = basis.astype(jnp.float32)

    def add_factor(total, pair):
        merged = merge(pair[0], pair[1]).astype(jnp.float32)
        return (total + jnp.einsum('lhd,lhr->ldr', merged, basis_wide, precision=lax.Precision.HIGHEST), None)
    start_factor = jnp.zeros((grads.shape[1], grads.shape[3], factor.shape[2]), jnp.float32)
    summed, _ = lax.scan(add_factor, start_factor, (grads, errors))
    factor_new = summed.astype(jnp.bfloat16)
    approx = jnp.einsum('lhr,ldr->lhd', basis_wide, factor_new.astype(jnp.float32), precision=lax.Precision.HIGHEST)

    def refresh(pair):
        merged = merge(pair[0], pair[1]).astype(jnp.float32)
        return (merged - approx / N_DP).astype(jnp.bfloat16)
    errors_new = lax.map(refresh, (grads, errors))
    return (errors_new, factor_new)

def reference(grad_query, grad_key, error_query, error_key, factor_query, factor_key):
    error_query_new, factor_query_new = compress(grad_query, error_query, factor_query)
    error_key_new, factor_key_new = compress(grad_key, error_key, factor_key)
    return (error_query_new, error_key_new, factor_query_new, factor_key_new)
```

```python
import functools

import jax
import jax.numpy as jnp
from jax import lax
from jax.experimental import pallas as pl
from jax.experimental.pallas import tpu as pltpu
from jax.sharding import PartitionSpec as P

F32, BF16 = jnp.float32, jnp.bfloat16
MIB = 1 << 20
EXACT = lax.Precision.HIGHEST
LANES = 128


def wide(a):
    return a.astype(F32)


def vmem(shape, dtype):
    return pltpu.VMEM(tuple(shape), dtype)


def whole():
    return pl.BlockSpec(memory_space=pltpu.VMEM)


def local(kernel, ins, outs, scratch=(), limit=8, flops=0, after=()):
    ins = [pltpu.with_memory_space_constraint(a, pltpu.VMEM) for a in ins]
    moved = sum(a.size * a.dtype.itemsize for a in ins)
    n_in, n_after = len(ins), len(after)

    def run(*refs):
        kernel(*refs[:n_in], *refs[n_in + n_after :])

    return pl.pallas_call(
        run,
        in_specs=[whole()] * n_in + [pl.BlockSpec(memory_space=pl.ANY)] * n_after,
        out_specs=[whole()] * len(outs),
        out_shape=list(outs),
        scratch_shapes=list(scratch),
        compiler_params=pltpu.CompilerParams(vmem_limit_bytes=limit * MIB),
        cost_estimate=pl.CostEstimate(flops=flops, bytes_accessed=moved, transcendentals=0),
    )(*ins, *after)


class Ring:
    def __init__(self, axis, total, stride, size):
        self.axis, self.total, self.stride, self.size = axis, total, stride, size
        self.pairwise = size & (size - 1) == 0

    def pos(self):
        return lax.rem(lax.div(lax.axis_index(self.axis), self.stride), self.size)

    def to(self, step):
        if self.pairwise:
            return lax.bitwise_xor(self.pos(), step)
        return lax.rem(self.pos() + step, self.size)

    def source(self, step):
        if self.pairwise:
            return lax.bitwise_xor(self.pos(), step)
        return lax.rem(self.pos() + (self.size - step), self.size)

    def send(self, x, step):
        pairs = []
        for src in range(self.total):
            p = (src // self.stride) % self.size
            q = p ^ step if self.pairwise else (p + step) % self.size
            pairs.append((src, src + (q - p) * self.stride))
        return lax.ppermute(x, self.axis, pairs)

    def scatter(self, parts):
        return [self.send(x, s + 1) for s, x in enumerate(parts)]

    def gather(self, x):
        return [self.send(x, s) for s in range(1, self.size)]


def rows_at(index, size, align):
    return pl.ds(pl.multiple_of(index * size, align), size)


def cut_into(held, base, share, ring, outs):
    size = share // ring.size
    for s, out in enumerate(outs):
        piece = held[pl.ds(pl.multiple_of(base + ring.to(s) * size, 8), size)]
        out[...] = piece.astype(out.dtype)


def image_kernel(rings, tile, depth, *refs):
    ins, outs, scratch = refs[:6], refs[6:-7], refs[-7:]
    grads, errors, factors = ins[0:2], ins[2:4], ins[4:6]
    merged, outs = outs[:2], outs[2:]
    arrived, flat_factors, natural, held, grad_sems, error_sems, factor_sems = scratch
    rank, d = flat_factors.shape[1:]
    tiles = [(m, i) for m in (0, 1) for i in range(grads[m].shape[0] // tile)]

    def copies(n):
        m, i = tiles[n]
        rows = pl.ds(i * tile, tile)
        return (
            pltpu.make_async_copy(grads[m].at[rows], merged[m].at[rows], grad_sems.at[n]),
            pltpu.make_async_copy(errors[m].at[rows], arrived.at[n], error_sems.at[n]),
        )

    def factor_copy(m):
        return pltpu.make_async_copy(factors[m], flat_factors.at[m], factor_sems.at[m])

    def start(n):
        for c in copies(n):
            c.start()

    factor_copy(0).start()
    for n in range(min(depth, len(tiles))):
        start(n)
        if n == 0:
            factor_copy(1).start()
    for m in range(2):
        factor_copy(m).wait()
        for t in range(0, d, LANES):
            natural[m, t : t + LANES] = wide(flat_factors[m, :, t : t + LANES]).T.astype(BF16)
    chunk = 512 if d % 512 == 0 else d
    for n, (m, i) in enumerate(tiles):
        for c in copies(n):
            c.wait()
        if n + depth < len(tiles):
            start(n + depth)
        rows = pl.ds(i * tile, tile)
        image = jnp.zeros((tile, rank), F32)
        for c in range(0, d, chunk):
            cols = pl.ds(c, chunk)
            x = (wide(merged[m][rows, cols]) + wide(arrived[n, :, cols])).astype(BF16)
            merged[m][rows, cols] = x
            image += jnp.dot(x, natural[m, cols], preferred_element_type=F32)
        held[n * rank : (n + 1) * rank] = image.T
    used = len(tiles) * rank
    if used < held.shape[0]:
        held[used:] = jnp.zeros((held.shape[0] - used, held.shape[1]), F32)
    share = held.shape[0] // len(rings)
    for r, ring in enumerate(rings):
        cut_into(held, r * share, share, ring, outs[: ring.size])
        outs = outs[ring.size :]


def images(rings, flat, grads, errors, factors):
    rows = [g.shape[0] for g in grads]
    d = grads[0].shape[1]
    rank = factors[0].shape[0]
    tile = LANES
    count = sum(rows) // tile
    ins = [pltpu.with_memory_space_constraint(a, pltpu.HBM) for a in (*grads, *errors, *factors)]
    outs = [vmem((r, d), BF16) for r in rows]
    for ring in rings:
        outs += [vmem((flat // len(rings) // ring.size, LANES), F32)] * ring.size
    got = pl.pallas_call(
        functools.partial(image_kernel, rings, tile, 4),
        in_specs=[pl.BlockSpec(memory_space=pltpu.HBM)] * len(ins),
        out_specs=[whole()] * len(outs),
        out_shape=outs,
        scratch_shapes=[
            vmem((count, tile, d), BF16),
            vmem((2, rank, d), BF16),
            vmem((2, d, rank), BF16),
            vmem((flat, LANES), F32),
            pltpu.SemaphoreType.DMA((count,)),
            pltpu.SemaphoreType.DMA((count,)),
            pltpu.SemaphoreType.DMA((2,)),
        ],
        compiler_params=pltpu.CompilerParams(vmem_limit_bytes=24 * MIB),
        cost_estimate=pl.CostEstimate(
            flops=2 * sum(rows) * d * 256, bytes_accessed=4 * sum(rows) * d, transcendentals=0
        ),
    )(*ins)
    merged, got = got[:2], list(got[2:])
    cuts = []
    for ring in rings:
        cuts.append((got[0], got[1 : ring.size]))
        got = got[ring.size :]
    return merged, cuts


def total_kernel(counts, *refs):
    ins, outs = list(refs[: sum(counts)]), refs[sum(counts) :]
    for count, out in zip(counts, outs):
        total = ins.pop(0)[...]
        for _ in range(count - 1):
            total = total + ins.pop(0)[...]
        out[...] = total


def assemble_kernel(rings, rank, rows, *refs):
    n_in = sum(r.size for r in rings)
    ins, (image_q, image_k, halves_q, halves_k, gram, held) = list(refs[:n_in]), refs[n_in:]
    share = held.shape[0] // len(rings)
    for r, ring in enumerate(rings):
        size = share // ring.size
        for s in range(ring.size):
            at = pl.multiple_of(r * share + ring.source(s) * size, 8)
            held[pl.ds(at, size)] = ins.pop(0)[...]
    n = 0
    for m, (image_out, halves) in enumerate(((image_q, halves_q), (image_k, halves_k))):
        count = rows[m] // LANES
        blocks = [held[(n + i) * rank : (n + i + 1) * rank] for i in range(count)]
        image = jnp.concatenate(blocks, axis=1) if count > 1 else blocks[0]
        n += count
        image_out[...] = image
        high = image.astype(BF16)
        halves[:rank] = high
        halves[rank:] = (image - wide(high)).astype(BF16)
        gram[:, m * rank : (m + 1) * rank] = lax.dot_general(
            image, image, (((1,), (1,)), ((), ())), precision=EXACT, preferred_element_type=F32
        )


def project_kernel(core, other, half, tile, halves_q, halves_k, merged_q, merged_k, out):
    rank = halves_q.shape[0] // 2
    d = merged_q.shape[1]
    first = (core.to(1) if other else core.pos()) * half
    for t in range(half // tile):
        start = first + t * tile

        def fill(start=start, t=t):
            cols = pl.ds(pl.multiple_of(start, tile), tile)
            both = []
            for halves, merged in ((halves_q, merged_q), (halves_k, merged_k)):
                p = jnp.dot(halves[...], merged[:, cols], preferred_element_type=F32)
                both.append(p[:rank] + p[rank:])
            p = jnp.concatenate(both, axis=0)
            out[t * tile : (t + 1) * tile] = p.T.astype(out.dtype)

        if 2 * half == d:
            fill()
        else:
            pl.when(start < d)(fill)

            @pl.when(start >= d)
            def _(t=t):
                out[t * tile : (t + 1) * tile] = jnp.zeros((tile, out.shape[1]), out.dtype)


def project(core, other, half, halves_q, halves_k, merged_q, merged_k):
    d = merged_q.shape[1]
    tile = 768 if half % 768 == 0 and d % 768 == 0 else LANES
    rows = merged_q.shape[0] + merged_k.shape[0]
    return local(
        functools.partial(project_kernel, core, other, half, tile),
        [halves_q, halves_k, merged_q, merged_k],
        [vmem((half, halves_q.shape[0]), BF16 if other else F32)],
        limit=16,
        flops=rows * d * 256,
    )[0]


def inverse_kernel(ring, *refs):
    grams, (out, held) = refs[:-2], refs[-2:]
    rank = out.shape[0] // 2
    for s, g in enumerate(grams):
        held[ring.source(s)] = g[...]
    lane = lax.broadcasted_iota(jnp.int32, (8, 2 * rank), 1)
    sub = lax.broadcasted_iota(jnp.int32, (8, 2 * rank), 0)
    both = held[0]
    for j in range(1, len(grams)):
        both += held[j]
    systems = []
    for m in range(2):
        gram = both[:, m * rank : (m + 1) * rank]
        gram = jnp.concatenate([gram, jnp.zeros((rank, rank), F32)], axis=1)
        systems.append(
            [
                jnp.where(lane == sub + (rank + 8 * i), 1.0, gram[8 * i : 8 * i + 8])
                for i in range(rank // 8)
            ]
        )
    for j in range(rank):
        i0, k = divmod(j, 8)
        for rows in systems:
            pivot = jnp.broadcast_to(rows[i0][k : k + 1, :], (8, 2 * rank))
            scaled = pivot * (1.0 / jnp.broadcast_to(pivot[:, j : j + 1], (8, 2 * rank)))
            for i in range(i0, rank // 8):
                updated = rows[i] - rows[i][:, j : j + 1] * scaled
                rows[i] = jnp.where(sub > k, updated, rows[i]) if i == i0 else updated
    for m, rows in enumerate(systems):
        for i, row in enumerate(rows):
            diagonal = jnp.where(lane == sub + 8 * i, row, 0.0).sum(axis=1, keepdims=True)
            right = row[:, rank:] / jnp.sqrt(diagonal)
            zero = jnp.zeros_like(right)
            pair = [right, zero] if m == 0 else [zero, right]
            out[m * rank + 8 * i : m * rank + 8 * i + 8] = jnp.concatenate(pair, axis=1)


def basis_kernel(scale, inverse, image_q, image_k, basis_q, basis_k):
    rank = image_q.shape[0]
    for m, (image, basis) in enumerate(((image_q, basis_q), (image_k, basis_k))):
        inv = inverse[m * rank : (m + 1) * rank, m * rank : (m + 1) * rank]
        b = jnp.dot(inv, image[...], precision=EXACT, preferred_element_type=F32)
        basis[...] = (wide(b.astype(BF16)) * scale).T.astype(BF16)


def split_kernel(jobs, *refs):
    n_in = sum(1 + j[0] for j in jobs)
    ins, outs = list(refs[:n_in]), list(refs[n_in : -len(jobs)])
    scratch = refs[-len(jobs) :]
    for (received, cuts), held in zip(jobs, scratch):
        total = ins.pop(0)[...]
        for _ in range(received):
            total = total + wide(ins.pop(0)[...])
        held[...] = total
        share = held.shape[0] // len(cuts)
        for r, ring in enumerate(cuts):
            cut_into(held, r * share, share, ring, outs[: ring.size])
            outs = outs[ring.size :]


def split(jobs, sent=BF16, after=()):
    ins, outs, scratch, plan = [], [], [], []
    for kept, received, cuts in jobs:
        ins += [kept] + list(received)
        plan.append((len(received), cuts))
        scratch.append(vmem(kept.shape, F32))
        for ring in cuts:
            shape = (kept.shape[0] // len(cuts) // ring.size, kept.shape[1])
            outs += [vmem(shape, F32)] + [vmem(shape, sent)] * (ring.size - 1)
    got = list(local(functools.partial(split_kernel, plan), ins, outs, scratch, limit=10, after=after))
    result = []
    for _, _, cuts in jobs:
        for ring in cuts:
            result.append((got[0], got[1 : ring.size]))
            got = got[ring.size :]
    return result


def split_two_kernel(received_a, received_b, ring, *refs):
    n_in = 2 + received_a + received_b
    ins, outs = refs[:n_in], refs[n_in:-2]
    held_a, held_b = refs[-2:]
    a = ins[0][...]
    for r in ins[1 : 1 + received_a]:
        a = a + wide(r[...])
    b = ins[1 + received_a][...]
    for r in ins[2 + received_a :]:
        b = b + wide(r[...])
    held_a[...] = a
    held_b[...] = b
    size = held_a.shape[0] // ring.size
    for s, out in enumerate(outs):
        at = rows_at(ring.to(s), size, 8)
        out[...] = jnp.concatenate([held_a[at], held_b[at]], axis=0).astype(out.dtype)


def finish_kernel(inverse, *refs):
    out = refs[-1]
    total = refs[0][...]
    for r in refs[1:-1]:
        total = total + wide(r[...])
    out[...] = lax.dot_general(
        total, inverse[...], (((1,), (1,)), ((), ())), precision=EXACT, preferred_element_type=F32
    ).astype(BF16)


def join_two_kernel(ring, *refs):
    parts, (out_a, out_b, held_a, held_b) = refs[:-4], refs[-4:]
    size = out_a.shape[0] // ring.size
    for s, r in enumerate(parts):
        both = wide(r[...])
        at = rows_at(ring.source(s), size, 8)
        held_a[at] = both[:size]
        held_b[at] = both[size:]
    out_a[...] = held_a[...].astype(BF16)
    out_b[...] = held_b[...].astype(BF16)


def join(rings, blocks):
    ins = [b for group in blocks for b in group]
    outs = [vmem((g[0].shape[0] * len(g), g[0].shape[1]), g[0].dtype) for g in blocks]
    return local(functools.partial(join_kernel, rings), ins, outs)


def join_kernel(rings, *refs):
    ins, outs = list(refs[: sum(r.size for r in rings)]), refs[sum(r.size for r in rings) :]
    for ring, out in zip(rings, outs):
        size = out.shape[0] // ring.size
        for s in range(ring.size):
            out[rows_at(ring.source(s), size, 8)] = ins.pop(0)[...]


def refresh_kernel(core, ring_a, ring_b, tiles_q, tile, *refs):
    n_pieces = 2 * (ring_a.size + ring_b.size)
    pieces = list(refs[:n_pieces])
    basis_q, basis_k, merged_q, merged_k, out_q, out_k, new_q, new_k, held, flat = refs[n_pieces:]
    rank, d = new_q.shape
    step = pl.program_id(0)
    half = held.shape[0] // 2

    @pl.when(step == 0)
    def _():
        for c in range(2):
            base = core.to(c) * half
            for ring in (ring_a, ring_b):
                size = half // 2 // ring.size
                for s in range(ring.size):
                    at = pl.multiple_of(base + ring.source(s) * size, 16)
                    held[pl.ds(at, size)] = pieces.pop(0)[...]
                base = base + half // 2
        for t in range(0, d, LANES):
            flat[:, t : t + LANES] = wide(held[t : t + LANES]).T.astype(BF16)
        new_q[...] = flat[:rank]
        new_k[...] = flat[rank:]

    chunk = 768 if d % 768 == 0 else d

    def update(at, merged, basis, factor, out):
        rows = rows_at(at, tile, tile)
        b = basis[rows]
        for c in range(0, d, chunk):
            approx = jnp.dot(b, factor[:, c : c + chunk], preferred_element_type=F32)
            out[:, c : c + chunk] = (wide(merged[rows, c : c + chunk]) - approx).astype(BF16)

    @pl.when(step < tiles_q)
    def _():
        update(step, merged_q, basis_q, flat.at[:rank], out_q)

    @pl.when(step >= tiles_q)
    def _():
        update(step - tiles_q, merged_k, basis_k, flat.at[rank:], out_k)


def refresh(core, ring_a, ring_b, padded, pieces, basis_q, basis_k, merged_q, merged_k):
    rank = basis_q.shape[1]
    rows_q, d = merged_q.shape
    rows_k = merged_k.shape[0]
    tile = 2 * LANES if rows_k % (2 * LANES) == 0 else LANES
    tiles_q, tiles_k = rows_q // tile, rows_k // tile
    ins = [*pieces, basis_q, basis_k, merged_q, merged_k]
    ins = [pltpu.with_memory_space_constraint(a, pltpu.VMEM) for a in ins]
    return pl.pallas_call(
        functools.partial(refresh_kernel, core, ring_a, ring_b, tiles_q, tile),
        grid=(tiles_q + tiles_k,),
        in_specs=[whole()] * len(ins),
        out_specs=[
            pl.BlockSpec((tile, d), lambda i: (jnp.minimum(i, tiles_q - 1), 0)),
            pl.BlockSpec((tile, d), lambda i: (jnp.maximum(i - tiles_q, 0), 0)),
            pl.BlockSpec((rank, d), lambda i: (0, 0)),
            pl.BlockSpec((rank, d), lambda i: (0, 0)),
        ],
        out_shape=[
            jax.ShapeDtypeStruct((rows_q, d), BF16),
            jax.ShapeDtypeStruct((rows_k, d), BF16),
            jax.ShapeDtypeStruct((rank, d), BF16),
            jax.ShapeDtypeStruct((rank, d), BF16),
        ],
        scratch_shapes=[vmem((padded, 2 * rank), BF16), vmem((2 * rank, d), BF16)],
        compiler_params=pltpu.CompilerParams(vmem_limit_bytes=24 * MIB),
        cost_estimate=pl.CostEstimate(
            flops=2 * (rows_q + rows_k) * d * 256, bytes_accessed=4 * (rows_q + rows_k) * d, transcendentals=0
        ),
    )(*ins)


def body(grad_query, grad_key, error_query, error_key, factor_query, factor_key):
    n_dp, n_t = lax.axis_size("dp"), lax.axis_size("tensor")
    n_z = 4 if n_dp % 4 == 0 else 2
    n_y = n_dp // n_z
    ring_y = Ring("dp", n_dp, 1, n_y)
    ring_z = Ring("dp", n_dp, n_y, n_z)
    core = Ring("tensor", n_t, 1, 2)
    ring_x = Ring("tensor", n_t, 2, n_t // 2)
    rows_q, d = grad_query.shape[2:]
    rows_k = grad_key.shape[2]
    rank = factor_query.shape[2]
    unit = 16 * n_dp * n_t
    padded = -(-d // unit) * unit
    half = padded // 2

    near, far = Ring("dp", n_dp, n_y, 2), Ring("dp", n_dp, 2 * n_y, n_z // 2)
    flat = -(-(rows_q + rows_k) // LANES * rank // (16 * n_dp)) * 16 * n_dp
    orders = [(ring_y, near, far), (near, far, ring_y)]
    (merged_q, merged_k), cuts = images(
        [o[0] for o in orders],
        flat,
        [grad_query[0, 0], grad_key[0, 0]],
        [error_query[0, 0], error_key[0, 0]],
        [factor_query[0].T, factor_key[0].T],
    )
    for level in range(1, 4):
        jobs = []
        for (kept, sent), order in zip(cuts, orders):
            got = order[level - 1].scatter(sent)
            jobs.append((kept, got, order[level : level + 1]))
        if level < 3:
            cuts = split(jobs, sent=F32)
    blocks = local(
        functools.partial(total_kernel, [1 + len(j[1]) for j in jobs]),
        [x for kept, got, _ in jobs for x in (kept, *got)],
        [vmem(kept.shape, F32) for kept, _, _ in jobs],
    )
    for level in (2, 1, 0):
        groups = [[b, *order[level].gather(b)] for b, order in zip(blocks, orders)]
        if level:
            blocks = join([order[level] for order in orders], groups)
    image_q, image_k, halves_q, halves_k, gram = local(
        functools.partial(assemble_kernel, [o[0] for o in orders], rank, (rows_q, rows_k)),
        [b for g in groups for b in g],
        [
            vmem((rank, rows_q), F32),
            vmem((rank, rows_k), F32),
            vmem((2 * rank, rows_q), BF16),
            vmem((2 * rank, rows_k), BF16),
            vmem((rank, 2 * rank), F32),
        ],
        [vmem((flat, LANES), F32)],
    )
    gram_pair = core.gather(gram)

    sent = project(core, True, half, halves_q, halves_k, merged_q, merged_k)
    got = core.scatter([sent])
    kept = project(core, False, half, halves_q, halves_k, merged_q, merged_k)
    gram = local(functools.partial(total_kernel, [2]), [gram, *gram_pair], [vmem(gram.shape, F32)])[0]
    grams = [gram, *ring_x.gather(gram)]
    (kept_a, sent_a), (kept_b, sent_b) = split([(kept, got, [ring_x, ring_y])])
    inverse = local(
        functools.partial(inverse_kernel, ring_x),
        grams,
        [vmem((2 * rank, 2 * rank), F32)],
        [vmem((len(grams), rank, 2 * rank), F32)],
        flops=1 << 32,
        after=[kept_a],
    )[0]
    got_a, got_b = ring_x.scatter(sent_a), ring_y.scatter(sent_b)
    (kept_a, sent_a), (kept_b, sent_b) = split(
        [(kept_a, got_a, [ring_y]), (kept_b, got_b, [ring_x])], after=[inverse]
    )
    got_a, got_b = ring_y.scatter(sent_a), ring_x.scatter(sent_b)
    piece = (2 * kept_a.shape[0] // n_z, 2 * rank)
    out = local(
        functools.partial(split_two_kernel, len(got_a), len(got_b), ring_z),
        [kept_a, *got_a, kept_b, *got_b],
        [vmem(piece, F32)] + [vmem(piece, BF16)] * (n_z - 1),
        [vmem(kept_a.shape, F32)] * 2,
    )
    got = ring_z.scatter(out[1:])
    own = local(finish_kernel, [inverse, out[0], *got], [vmem(piece, BF16)])[0]

    got = ring_z.gather(own)
    part = (kept_a.shape[0], 2 * rank)
    own_a, own_b = local(
        functools.partial(join_two_kernel, ring_z), [own, *got], [vmem(part, BF16)] * 2, [vmem(part, F32)] * 2
    )
    all_a, all_b = ring_y.gather(own_a), ring_x.gather(own_b)
    own_a, own_b = join([ring_y, ring_x], [[own_a, *all_a], [own_b, *all_b]])
    pieces = [own_a, *ring_x.gather(own_a), own_b, *ring_y.gather(own_b)]
    pieces += [core.send(p, 1) for p in pieces]
    basis_q, basis_k = local(
        functools.partial(basis_kernel, 1.0 / n_dp),
        [inverse, image_q, image_k],
        [vmem((rows_q, rank), BF16), vmem((rows_k, rank), BF16)],
    )
    error_q, error_k, new_q, new_k = refresh(
        core, ring_x, ring_y, padded, pieces, basis_q, basis_k, merged_q, merged_k
    )
    return error_q[None, None], error_k[None, None], new_q.T[None], new_k.T[None]


def solution(mesh):
    rows = P("dp", None, "tensor", None)
    return jax.shard_map(
        body,
        mesh=mesh,
        in_specs=(rows, rows, rows, rows, P(), P()),
        out_specs=(rows, rows, P(), P()),
        check_vma=False,
    )
```

```python
import functools

import jax
import jax.numpy as jnp
from jax import lax
from jax.experimental import pallas as pl
from jax.experimental.pallas import tpu as pltpu
from jax.sharding import Mesh, PartitionSpec as P

F32, BF16 = jnp.float32, jnp.bfloat16
MIB = 1 << 20
AXES = ("z", "y", "x", "core")
EXACT = lax.Precision.HIGHEST
LANES = 128


def wide(a):
    return a.astype(F32)


def vmem(shape, dtype):
    return pltpu.VMEM(tuple(shape), dtype)


def whole():
    return pl.BlockSpec(memory_space=pltpu.VMEM)


def local(kernel, ins, outs, scratch=(), limit=8, flops=0, after=()):
    ins = [pltpu.with_memory_space_constraint(a, pltpu.VMEM) for a in ins]
    moved = sum(a.size * a.dtype.itemsize for a in ins)
    n_in, n_after = len(ins), len(after)

    def run(*refs):
        kernel(*refs[:n_in], *refs[n_in + n_after :])

    return pl.pallas_call(
        run,
        in_specs=[whole()] * n_in + [pl.BlockSpec(memory_space=pl.ANY)] * n_after,
        out_specs=[whole()] * len(outs),
        out_shape=list(outs),
        scratch_shapes=list(scratch),
        compiler_params=pltpu.CompilerParams(vmem_limit_bytes=limit * MIB),
        cost_estimate=pl.CostEstimate(flops=flops, bytes_accessed=moved, transcendentals=0),
    )(*ins, *after)


class Group:
    def __init__(self, digits, count):
        self.digits, self.count = digits, count
        self.size = 1
        for _, size in digits:
            self.size *= size
        self.pairwise = self.size & (self.size - 1) == 0

    def place(self, index):
        p, weight = 0, 1
        for stride, size in self.digits:
            p = p + (index // stride) % size * weight
            weight *= size
        return p

    def pos(self):
        p, weight = 0, 1
        index = lax.axis_index(AXES)
        for stride, size in self.digits:
            p = p + lax.rem(lax.div(index, stride), size) * weight
            weight *= size
        return p

    def to(self, step):
        if self.pairwise:
            return lax.bitwise_xor(self.pos(), step)
        return lax.rem(self.pos() + step, self.size)

    def source(self, step):
        if self.pairwise:
            return lax.bitwise_xor(self.pos(), step)
        return lax.rem(self.pos() + (self.size - step), self.size)

    def send(self, x, step):
        pairs = []
        for src in range(self.count):
            p = self.place(src)
            q = p ^ step if self.pairwise else (p + step) % self.size
            dst, weight = src, 1
            for stride, size in self.digits:
                dst += ((q // weight) % size - (p // weight) % size) * stride
                weight *= size
            pairs.append((src, dst))
        return lax.ppermute(x, AXES, pairs)

    def scatter(self, parts):
        return [self.send(x, s + 1) for s, x in enumerate(parts)]

    def gather(self, x):
        return [self.send(x, s) for s in range(1, self.size)]


def rows_at(index, size, align):
    return pl.ds(pl.multiple_of(index * size, align), size)


def blocks_at(group, size, align):
    return [rows_at(group.source(s), size, align) for s in range(group.size)]


def cut_into(held, group, outs):
    size = held.shape[0] // group.size
    for s, out in enumerate(outs):
        out[...] = held[rows_at(group.to(s), size, 8)].astype(out.dtype)


def image_kernel(tile, depth, *refs):
    ins, outs, scratch = refs[:6], refs[6:9], refs[9:]
    grads, errors, factors = ins[0:2], ins[2:4], ins[4:6]
    merged, held = outs[:2], outs[2]
    arrived, flat_factors, natural, grad_sems, error_sems, factor_sems = scratch
    rank, d = flat_factors.shape[1:]
    tiles = [(m, i) for m in (0, 1) for i in range(grads[m].shape[0] // tile)]

    def copies(n):
        m, i = tiles[n]
        rows = pl.ds(i * tile, tile)
        return (
            pltpu.make_async_copy(grads[m].at[rows], merged[m].at[rows], grad_sems.at[n]),
            pltpu.make_async_copy(errors[m].at[rows], arrived.at[n], error_sems.at[n]),
        )

    def factor_copy(m):
        return pltpu.make_async_copy(factors[m], flat_factors.at[m], factor_sems.at[m])

    def start(n):
        for c in copies(n):
            c.start()

    factor_copy(0).start()
    for n in range(min(depth, len(tiles))):
        start(n)
        if n == 0:
            factor_copy(1).start()
    for m in range(2):
        factor_copy(m).wait()
        for t in range(0, d, LANES):
            natural[m, t : t + LANES] = wide(flat_factors[m, :, t : t + LANES]).T.astype(BF16)
    chunk = 512 if d % 512 == 0 else d
    for n, (m, i) in enumerate(tiles):
        for c in copies(n):
            c.wait()
        if n + depth < len(tiles):
            start(n + depth)
        rows = pl.ds(i * tile, tile)
        image = jnp.zeros((tile, rank), F32)
        for c in range(0, d, chunk):
            cols = pl.ds(c, chunk)
            x = (wide(merged[m][rows, cols]) + wide(arrived[n, :, cols])).astype(BF16)
            merged[m][rows, cols] = x
            image += jnp.dot(x, natural[m, cols], preferred_element_type=F32)
        held[n * rank : (n + 1) * rank] = image.T.astype(BF16)
    used = len(tiles) * rank
    if used < held.shape[0]:
        held[used:] = jnp.zeros((held.shape[0] - used, held.shape[1]), BF16)


def images(flat, grads, errors, factors):
    rows = [g.shape[0] for g in grads]
    d = grads[0].shape[1]
    rank = factors[0].shape[0]
    tile = LANES
    count = sum(rows) // tile
    ins = [pltpu.with_memory_space_constraint(a, pltpu.HBM) for a in (*grads, *errors, *factors)]
    outs = [vmem((r, d), BF16) for r in rows] + [vmem((flat, LANES), BF16)]
    return pl.pallas_call(
        functools.partial(image_kernel, tile, 6),
        in_specs=[pl.BlockSpec(memory_space=pltpu.HBM)] * len(ins),
        out_specs=[whole()] * len(outs),
        out_shape=outs,
        scratch_shapes=[
            vmem((count, tile, d), BF16),
            vmem((2, rank, d), BF16),
            vmem((2, d, rank), BF16),
            pltpu.SemaphoreType.DMA((count,)),
            pltpu.SemaphoreType.DMA((count,)),
            pltpu.SemaphoreType.DMA((2,)),
        ],
        compiler_params=pltpu.CompilerParams(vmem_limit_bytes=24 * MIB),
        cost_estimate=pl.CostEstimate(
            flops=2 * sum(rows) * d * 256, bytes_accessed=4 * sum(rows) * d, transcendentals=0
        ),
    )(*ins)


def share_total_kernel(blocks, copies):
    total = wide(blocks[0])
    for s in range(1, blocks.shape[0]):
        total = total + wide(blocks[s])
    for s in range(copies.shape[0]):
        copies[s] = total.astype(BF16)


def total_kernel(a, b, out):
    out[...] = a[...] + b[...]


def assemble_kernel(rank, rows, flat, image_q, image_k, gram):
    n = 0
    for m, image_out in enumerate((image_q, image_k)):
        count = rows[m] // LANES
        blocks = [flat[(n + i) * rank : (n + i + 1) * rank] for i in range(count)]
        image = jnp.concatenate(blocks, axis=1) if count > 1 else blocks[0]
        n += count
        image_out[...] = image
        gram[:, m * rank : (m + 1) * rank] = lax.dot_general(
            image, image, (((1,), (1,)), ((), ())), preferred_element_type=F32
        )


def project_kernel(core, other, tile, image_q, image_k, merged_q, merged_k, out):
    d = merged_q.shape[1]
    half = out.shape[0]
    first = (core.to(1) if other else core.pos()) * half
    for t in range(0, half, tile):
        start = pl.multiple_of(first + t, LANES)

        def fill(start=start, t=t):
            both = [
                jnp.dot(image[...], merged[:, pl.ds(start, tile)], preferred_element_type=F32)
                for image, merged in ((image_q, merged_q), (image_k, merged_k))
            ]
            out[t : t + tile] = jnp.concatenate(both, axis=0).T.astype(out.dtype)

        if 2 * half == d:
            fill()
        else:
            pl.when(start < d)(fill)

            @pl.when(start >= d)
            def _(t=t):
                out[t : t + tile] = jnp.zeros((tile, out.shape[1]), out.dtype)


def project(core, other, half, image_q, image_k, merged_q, merged_k):
    d = merged_q.shape[1]
    tile = next(t for t in (768, 512, 256, 128) if half % t == 0 and d % t == 0)
    return local(
        functools.partial(project_kernel, core, other, tile),
        [image_q, image_k, merged_q, merged_k],
        [vmem((half, 2 * image_q.shape[0]), BF16 if other else F32)],
        limit=16,
        flops=(merged_q.shape[0] + merged_k.shape[0]) * half * 512,
    )[0]


def inverse_kernel(group, *refs):
    grams, (out, held) = refs[:-2], refs[-2:]
    rank = out.shape[0] // 2
    for s, g in enumerate(grams):
        held[group.source(s)] = g[...]
    lane = lax.broadcasted_iota(jnp.int32, (8, 2 * rank), 1)
    sub = lax.broadcasted_iota(jnp.int32, (8, 2 * rank), 0)
    both = held[0]
    for j in range(1, len(grams)):
        both += held[j]
    systems = []
    for m in range(2):
        gram = both[:, m * rank : (m + 1) * rank]
        gram = jnp.concatenate([gram, jnp.zeros((rank, rank), F32)], axis=1)
        systems.append(
            [
                jnp.where(lane == sub + (rank + 8 * i), 1.0, gram[8 * i : 8 * i + 8])
                for i in range(rank // 8)
            ]
        )
    shape = (8, 2 * rank)
    results = [[None] * (rank // 8) for _ in systems]
    for j in range(0, rank, 2):
        i0, k = divmod(j, 8)
        for m, rows in enumerate(systems):
            one = jnp.broadcast_to(rows[i0][k : k + 1, :], shape)
            two = jnp.broadcast_to(rows[i0][k + 1 : k + 2, :], shape)
            a = jnp.broadcast_to(one[:, j : j + 1], shape)
            b = jnp.broadcast_to(one[:, j + 1 : j + 2], shape)
            c = jnp.broadcast_to(two[:, j + 1 : j + 2], shape)
            det = 1.0 / (a * c - b * b)
            first, second = (c * one - b * two) * det, (a * two - b * one) * det
            ratio = b / a
            done = results[m][i0] if k else jnp.zeros(shape, F32)
            done = jnp.where(sub == k, one / jnp.sqrt(a), done)
            below = (two - ratio * one) / jnp.sqrt(c - ratio * b)
            results[m][i0] = jnp.where(sub == k + 1, below, done)
            for i in range(i0 if k < 6 else i0 + 1, rank // 8):
                x = rows[i]
                rows[i] = x - x[:, j : j + 1] * first - x[:, j + 1 : j + 2] * second
    for m, rows in enumerate(results):
        for i, row in enumerate(rows):
            right = row[:, rank:]
            zero = jnp.zeros_like(right)
            pair = [right, zero] if m == 0 else [zero, right]
            out[m * rank + 8 * i : m * rank + 8 * i + 8] = jnp.concatenate(pair, axis=1)


def basis_kernel(scale, inverse, image_q, image_k, basis_q, basis_k):
    rank = image_q.shape[0]
    for m, (image, basis) in enumerate(((image_q, basis_q), (image_k, basis_k))):
        inv = inverse[m * rank : (m + 1) * rank, m * rank : (m + 1) * rank]
        b = jnp.dot(inv, wide(image[...]), precision=EXACT, preferred_element_type=F32)
        basis[...] = (wide(b.astype(BF16)) * scale).T.astype(BF16)


def split_kernel(group, *refs):
    ins, (kept, *sent), held = refs[: -group.size - 1], refs[-group.size - 1 : -1], refs[-1]
    total = ins[0][...]
    for r in ins[1:]:
        total = total + wide(r[...])
    held[...] = total
    cut_into(held, group, [kept, *sent])


def split(kept, received, group):
    rows, width = kept.shape
    shape = (rows // group.size, width)
    got = local(
        functools.partial(split_kernel, group),
        [kept, *received],
        [vmem(shape, F32)] + [vmem(shape, BF16)] * (group.size - 1),
        [vmem((rows, width), F32)],
    )
    return got[0], got[1:]


def stack_kernel(*refs):
    ins, out = refs[:-1], refs[-1]
    total = ins[0][...]
    for r in ins[1:]:
        total = total + wide(r[...])
    for s in range(out.shape[0]):
        out[s] = total[s * out.shape[1] : (s + 1) * out.shape[1]].astype(BF16)


def finish_kernel(inverse, blocks, copies):
    total = wide(blocks[0])
    for s in range(1, blocks.shape[0]):
        total = total + wide(blocks[s])
    new = lax.dot_general(
        total, inverse[...], (((1,), (1,)), ((), ())), precision=EXACT, preferred_element_type=F32
    ).astype(BF16)
    for s in range(copies.shape[0]):
        copies[s] = new


def copies_kernel(x, copies):
    for s in range(copies.shape[0]):
        copies[s] = x[...]


def refresh_kernel(core, tiles_q, tile, *refs):
    own, other, basis_q, basis_k, merged_q, merged_k, out_q, out_k, new_q, new_k, held, flat = refs
    rank, d = new_q.shape
    step = pl.program_id(0)

    @pl.when(step == 0)
    def _():
        half = held.shape[0] // 2
        held[rows_at(core.pos(), half, 16)] = own[...]
        held[rows_at(core.to(1), half, 16)] = other[...]
        for t in range(0, d, LANES):
            flat[:, t : t + LANES] = wide(held[t : t + LANES]).T.astype(BF16)
        new_q[...] = flat[:rank]
        new_k[...] = flat[rank:]

    chunk = 768 if d % 768 == 0 else d

    def update(at, merged, basis, factor, out):
        rows = rows_at(at, tile, tile)
        b = basis[rows]
        for c in range(0, d, chunk):
            approx = jnp.dot(b, factor[:, c : c + chunk], preferred_element_type=F32)
            out[:, c : c + chunk] = (wide(merged[rows, c : c + chunk]) - approx).astype(BF16)

    @pl.when(step < tiles_q)
    def _():
        update(step, merged_q, basis_q, flat.at[:rank], out_q)

    @pl.when(step >= tiles_q)
    def _():
        update(step - tiles_q, merged_k, basis_k, flat.at[rank:], out_k)


def refresh(core, padded, pieces, basis_q, basis_k, merged_q, merged_k):
    rank = basis_q.shape[1]
    rows_q, d = merged_q.shape
    rows_k = merged_k.shape[0]
    tile = 2 * LANES if rows_k % (2 * LANES) == 0 else LANES
    tiles_q, tiles_k = rows_q // tile, rows_k // tile
    ins = [*pieces, basis_q, basis_k, merged_q, merged_k]
    ins = [pltpu.with_memory_space_constraint(a, pltpu.VMEM) for a in ins]
    return pl.pallas_call(
        functools.partial(refresh_kernel, core, tiles_q, tile),
        grid=(tiles_q + tiles_k,),
        in_specs=[whole()] * len(ins),
        out_specs=[
            pl.BlockSpec((tile, d), lambda i: (jnp.minimum(i, tiles_q - 1), 0)),
            pl.BlockSpec((tile, d), lambda i: (jnp.maximum(i - tiles_q, 0), 0)),
            pl.BlockSpec((rank, d), lambda i: (0, 0)),
            pl.BlockSpec((rank, d), lambda i: (0, 0)),
        ],
        out_shape=[
            jax.ShapeDtypeStruct((rows_q, d), BF16),
            jax.ShapeDtypeStruct((rows_k, d), BF16),
            jax.ShapeDtypeStruct((rank, d), BF16),
            jax.ShapeDtypeStruct((rank, d), BF16),
        ],
        scratch_shapes=[vmem((padded, 2 * rank), BF16), vmem((2 * rank, d), BF16)],
        compiler_params=pltpu.CompilerParams(vmem_limit_bytes=24 * MIB),
        cost_estimate=pl.CostEstimate(
            flops=2 * (rows_q + rows_k) * d * 256, bytes_accessed=4 * (rows_q + rows_k) * d, transcendentals=0
        ),
    )(*ins)


def body(grad_query, grad_key, error_query, error_key, factor_query, factor_key):
    n_z, n_y, n_x, n_core = (lax.axis_size(a) for a in AXES)
    n_dp, count = n_z * n_y, n_z * n_y * n_x * n_core
    core = Group([(1, n_core)], count)
    across = Group([(n_core, n_x)], count)
    plane = Group([(n_core, n_x), (n_core * n_x, n_y)], count)
    rows_q, d = grad_query.shape[2:]
    rows_k = grad_key.shape[2]
    rank = factor_query.shape[2]
    unit = 16 * count
    padded = -(-d // unit) * unit
    half = padded // 2

    flat = -(-((rows_q + rows_k) // LANES * rank) // (16 * n_dp)) * 16 * n_dp
    merged_q, merged_k, blocks = images(
        flat,
        [grad_query[0, 0], grad_key[0, 0]],
        [error_query[0, 0], error_key[0, 0]],
        [factor_query[0].T, factor_key[0].T],
    )
    blocks = blocks.reshape(n_dp, flat // n_dp, LANES)
    blocks = lax.all_to_all(blocks, ("z", "y"), 0, 0)
    blocks = local(share_total_kernel, [blocks], [vmem(blocks.shape, BF16)])[0]
    blocks = lax.all_to_all(blocks, ("z", "y"), 0, 0)
    image_q, image_k, gram = local(
        functools.partial(assemble_kernel, rank, (rows_q, rows_k)),
        [blocks.reshape(flat, LANES)],
        [vmem((rank, rows_q), BF16), vmem((rank, rows_k), BF16), vmem((rank, 2 * rank), F32)],
    )

    gram_pair = core.send(gram, 1)
    operands = (image_q, image_k, merged_q, merged_k)
    got = core.send(project(core, True, half, *operands), 1)
    kept = project(core, False, half, *operands)
    gram = local(total_kernel, [gram, gram_pair], [vmem(gram.shape, F32)])[0]
    grams = [gram, *across.gather(gram)]
    kept, sent = split(kept, [got], plane)
    inverse = local(
        functools.partial(inverse_kernel, across),
        grams,
        [vmem((2 * rank, 2 * rank), F32)],
        [vmem((len(grams), rank, 2 * rank), F32)],
        flops=1 << 32,
        after=[kept],
    )[0]
    basis_q, basis_k = local(
        functools.partial(basis_kernel, 1.0 / n_dp),
        [inverse, image_q, image_k],
        [vmem((rows_q, rank), BF16), vmem((rows_k, rank), BF16)],
    )
    piece = (kept.shape[0] // n_z, kept.shape[1])
    blocks = local(
        stack_kernel, [kept, *plane.scatter(sent)], [vmem((n_z,) + piece, BF16)], after=[basis_k]
    )[0]
    blocks = lax.all_to_all(blocks, "z", 0, 0)
    blocks = local(finish_kernel, [inverse, blocks], [vmem(blocks.shape, BF16)])[0]

    blocks = lax.all_to_all(blocks, "z", 0, 0).reshape(kept.shape)
    copies = local(copies_kernel, [blocks], [vmem((plane.size,) + blocks.shape, BF16)])[0]
    own = lax.all_to_all(copies, ("y", "x"), 0, 0).reshape(half, 2 * rank)
    pieces = [own, core.send(own, 1)]
    error_q, error_k, new_q, new_k = refresh(
        core, padded, pieces, basis_q, basis_k, merged_q, merged_k
    )
    return error_q[None, None], error_k[None, None], new_q.T[None], new_k.T[None]


def solution(mesh):
    n_dp, n_t = mesh.shape["dp"], mesh.shape["tensor"]
    n_z = 4 if n_dp % 4 == 0 else 1
    chips = Mesh(mesh.devices.reshape(n_z, n_dp // n_z, n_t // 2, 2), AXES)
    rows = P(("z", "y"), None, ("x", "core"), None)
    return jax.shard_map(
        body,
        mesh=chips,
        in_specs=(rows, rows, rows, rows, P(), P()),
        out_specs=(rows, rows, P(), P()),
        check_vma=False,
    )
```

```python
import functools

import jax
import jax.numpy as jnp
from jax import lax
from jax.experimental import pallas as pl
from jax.experimental.pallas import tpu as pltpu
from jax.sharding import Mesh, PartitionSpec as P

F32, BF16 = jnp.float32, jnp.bfloat16
MIB = 1 << 20
AXES = ("z", "y", "x", "core")
LIMIT = 3.0
EXACT = lax.Precision.HIGHEST
LANES = 128


def wide(a):
    return a.astype(F32)


def vmem(shape, dtype):
    return pltpu.VMEM(tuple(shape), dtype)


def whole():
    return pl.BlockSpec(memory_space=pltpu.VMEM)


def local(kernel, ins, outs, scratch=(), limit=8, flops=0, after=()):
    ins = [pltpu.with_memory_space_constraint(a, pltpu.VMEM) for a in ins]
    moved = sum(a.size * a.dtype.itemsize for a in ins)
    n_in, n_after = len(ins), len(after)

    def run(*refs):
        kernel(*refs[:n_in], *refs[n_in + n_after :])

    return pl.pallas_call(
        run,
        in_specs=[whole()] * n_in + [pl.BlockSpec(memory_space=pl.ANY)] * n_after,
        out_specs=[pl.BlockSpec(memory_space=o.memory_space) for o in outs],
        out_shape=list(outs),
        scratch_shapes=list(scratch),
        compiler_params=pltpu.CompilerParams(vmem_limit_bytes=limit * MIB),
        cost_estimate=pl.CostEstimate(flops=flops, bytes_accessed=moved, transcendentals=0),
    )(*ins, *after)


class Group:
    def __init__(self, digits, count):
        self.digits, self.count = digits, count
        self.size = 1
        for _, size in digits:
            self.size *= size
        self.pairwise = self.size & (self.size - 1) == 0

    def place(self, index):
        p, weight = 0, 1
        for stride, size in self.digits:
            p = p + (index // stride) % size * weight
            weight *= size
        return p

    def pos(self):
        p, weight = 0, 1
        index = lax.axis_index(AXES)
        for stride, size in self.digits:
            p = p + lax.rem(lax.div(index, stride), size) * weight
            weight *= size
        return p

    def to(self, step):
        if self.pairwise:
            return lax.bitwise_xor(self.pos(), step)
        return lax.rem(self.pos() + step, self.size)

    def source(self, step):
        if self.pairwise:
            return lax.bitwise_xor(self.pos(), step)
        return lax.rem(self.pos() + (self.size - step), self.size)

    def send(self, x, step):
        pairs = []
        for src in range(self.count):
            p = self.place(src)
            q = p ^ step if self.pairwise else (p + step) % self.size
            dst, weight = src, 1
            for stride, size in self.digits:
                dst += ((q // weight) % size - (p // weight) % size) * stride
                weight *= size
            pairs.append((src, dst))
        return lax.ppermute(x, AXES, pairs)

    def scatter(self, parts):
        return [self.send(x, s + 1) for s, x in enumerate(parts)]

    def gather(self, x):
        return [self.send(x, s) for s in range(1, self.size)]


def rows_at(index, size, align):
    return pl.ds(pl.multiple_of(index * size, align), size)


def blocks_at(group, size, align):
    return [rows_at(group.source(s), size, align) for s in range(group.size)]


def cut_into(held, group, outs):
    size = held.shape[0] // group.size
    for s, out in enumerate(outs):
        out[...] = held[rows_at(group.to(s), size, 8)].astype(out.dtype)


def image_kernel(group, tile, depth, *refs):
    ins, merged, outs, scratch = refs[:6], refs[6:8], refs[8 : 8 + group.size], refs[8 + group.size :]
    grads, errors, factors = ins[0:2], ins[2:4], ins[4:6]
    arrived, flat_factors, natural, held, grad_sems, error_sems, factor_sems = scratch
    rank, d = flat_factors.shape[1:]
    tiles = [(m, i) for m in (0, 1) for i in range(grads[m].shape[0] // tile)]

    def copies(n):
        m, i = tiles[n]
        rows = pl.ds(i * tile, tile)
        return (
            pltpu.make_async_copy(grads[m].at[rows], merged[m].at[rows], grad_sems.at[n]),
            pltpu.make_async_copy(errors[m].at[rows], arrived.at[n], error_sems.at[n]),
        )

    def factor_copy(m):
        return pltpu.make_async_copy(factors[m], flat_factors.at[m], factor_sems.at[m])

    def start(n):
        for c in copies(n):
            c.start()

    factor_copy(0).start()
    for n in range(min(depth, len(tiles))):
        start(n)
        if n == 0:
            factor_copy(1).start()
    for m in range(2):
        factor_copy(m).wait()
        for t in range(0, d, LANES):
            natural[m, t : t + LANES] = wide(flat_factors[m, :, t : t + LANES]).T.astype(BF16)
    chunk = 512 if d % 512 == 0 else d
    for n, (m, i) in enumerate(tiles):
        for c in copies(n):
            c.wait()
        if n + depth < len(tiles):
            start(n + depth)
        rows = pl.ds(i * tile, tile)
        image = jnp.zeros((tile, rank), F32)
        for c in range(0, d, chunk):
            cols = pl.ds(c, chunk)
            x = (wide(merged[m][rows, cols]) + wide(arrived[n, :, cols])).astype(BF16)
            merged[m][rows, cols] = x
            image += jnp.dot(x, natural[m, cols], preferred_element_type=F32)
        held[n * rank : (n + 1) * rank] = image.T
    used = len(tiles) * rank
    if used < held.shape[0]:
        held[used:] = jnp.zeros((held.shape[0] - used, held.shape[1]), F32)
    cut_into(held, group, outs)


def images(group, flat, grads, errors, factors):
    rows = [g.shape[0] for g in grads]
    d = grads[0].shape[1]
    rank = factors[0].shape[0]
    tile = LANES
    count = sum(rows) // tile
    ins = [pltpu.with_memory_space_constraint(a, pltpu.HBM) for a in (*grads, *errors, *factors)]
    cut = (flat // group.size, LANES)
    outs = [vmem((r, d), BF16) for r in rows] + [vmem(cut, F32)] + [vmem(cut, BF16)] * (group.size - 1)
    return pl.pallas_call(
        functools.partial(image_kernel, group, tile, 2),
        in_specs=[pl.BlockSpec(memory_space=pltpu.HBM)] * len(ins),
        out_specs=[whole()] * len(outs),
        out_shape=outs,
        scratch_shapes=[
            vmem((count, tile, d), BF16),
            vmem((2, rank, d), BF16),
            vmem((2, d, rank), BF16),
            vmem((flat, LANES), F32),
            pltpu.SemaphoreType.DMA((count,)),
            pltpu.SemaphoreType.DMA((count,)),
            pltpu.SemaphoreType.DMA((2,)),
        ],
        compiler_params=pltpu.CompilerParams(vmem_limit_bytes=24 * MIB),
        cost_estimate=pl.CostEstimate(
            flops=2 * sum(rows) * d * 256, bytes_accessed=4 * sum(rows) * d, transcendentals=0
        ),
    )(*ins)


def ordered_kernel(group, *refs):
    blocks, (out, held) = refs[:-2], refs[-2:]
    for s, block in enumerate(blocks):
        held[group.source(s)] = wide(block[...])
    total = held[0]
    for j in range(1, len(blocks)):
        total = total + held[j]
    out[...] = total.astype(BF16)


def assemble_kernel(group, rank, rows, *refs):
    blocks, (image_q, image_k, gram, flat) = refs[: group.size], refs[group.size :]
    for s, block in enumerate(blocks):
        size = block.shape[0]
        flat[rows_at(group.source(s), size, 16)] = block[...]
    n = 0
    for m, image_out in enumerate((image_q, image_k)):
        count = rows[m] // LANES
        parts = [flat[(n + i) * rank : (n + i + 1) * rank] for i in range(count)]
        image = jnp.concatenate(parts, axis=1) if count > 1 else parts[0]
        n += count
        image_out[...] = image
        gram[:, m * rank : (m + 1) * rank] = lax.dot_general(
            image, image, (((1,), (1,)), ((), ())), preferred_element_type=F32
        )


def project_kernel(core, other, tile, image_q, image_k, merged_q, merged_k, out):
    d = merged_q.shape[1]
    half = out.shape[0]
    first = (core.to(1) if other else core.pos()) * half
    for t in range(0, half, tile):
        start = pl.multiple_of(first + t, LANES)

        def fill(start=start, t=t):
            both = [
                jnp.dot(image[...], merged[:, pl.ds(start, tile)], preferred_element_type=F32)
                for image, merged in ((image_q, merged_q), (image_k, merged_k))
            ]
            out[t : t + tile] = jnp.concatenate(both, axis=0).T.astype(out.dtype)

        if 2 * half == d:
            fill()
        else:
            pl.when(start < d)(fill)

            @pl.when(start >= d)
            def _(t=t):
                out[t : t + tile] = jnp.zeros((tile, out.shape[1]), out.dtype)


def project(core, other, half, image_q, image_k, merged_q, merged_k):
    d = merged_q.shape[1]
    tile = next(t for t in (768, 512, 256, 128) if half % t == 0 and d % t == 0)
    return local(
        functools.partial(project_kernel, core, other, tile),
        [image_q, image_k, merged_q, merged_k],
        [vmem((half, 2 * image_q.shape[0]), BF16 if other else F32)],
        limit=16,
        flops=(merged_q.shape[0] + merged_k.shape[0]) * half * 512,
    )[0]


def parts_of(x):
    high = x.astype(BF16)
    rest = x - wide(high)
    middle = rest.astype(BF16)
    return high, middle, (rest - wide(middle)).astype(BF16)


def inverse_kernel(group, own, *refs):
    received, (out, growth, held) = refs[:-3], refs[-3:]
    rank = out.shape[0] // 2
    tail = slice(received[0].shape[0] - 3 * rank, None)
    for s, three in enumerate([parts_of(own[...])] + [r[tail] for r in received]):
        if s:
            three = [three[i * rank : (i + 1) * rank] for i in range(3)]
        high, middle, low = (wide(p) for p in three)
        held[group.source(s)] = high + (middle + low)
    lane = lax.broadcasted_iota(jnp.int32, (8, 2 * rank), 1)
    sub = lax.broadcasted_iota(jnp.int32, (8, 2 * rank), 0)
    both = held[0]
    for j in range(1, group.size):
        both += held[j]
    systems = []
    for m in range(2):
        gram = both[:, m * rank : (m + 1) * rank]
        gram = jnp.concatenate([gram, jnp.zeros((rank, rank), F32)], axis=1)
        systems.append(
            [
                jnp.where(lane == sub + (rank + 8 * i), 1.0, gram[8 * i : 8 * i + 8])
                for i in range(rank // 8)
            ]
        )
    shape = (8, 2 * rank)
    square = lax.broadcasted_iota(jnp.int32, both.shape, 0) - lax.broadcasted_iota(jnp.int32, both.shape, 1)
    norms = jnp.where((square == 0) | (square == -rank), both, 0.0).sum(axis=0, keepdims=True)
    worse = jnp.zeros((8, 1), F32)
    results = [[None] * (rank // 8) for _ in systems]
    for j in range(0, rank, 2):
        i0, k = divmod(j, 8)
        for m, rows in enumerate(systems):
            one = jnp.broadcast_to(rows[i0][k : k + 1, :], shape)
            two = jnp.broadcast_to(rows[i0][k + 1 : k + 2, :], shape)
            a = jnp.broadcast_to(one[:, j : j + 1], shape)
            b = jnp.broadcast_to(one[:, j + 1 : j + 2], shape)
            c = jnp.broadcast_to(two[:, j + 1 : j + 2], shape)
            det = 1.0 / (a * c - b * b)
            first, second = (c * one - b * two) * det, (a * two - b * one) * det
            ratio = b / a
            done = results[m][i0] if k else jnp.zeros(shape, F32)
            done = jnp.where(sub == k, one / jnp.sqrt(a), done)
            below = (two - ratio * one) / jnp.sqrt(c - ratio * b)
            results[m][i0] = jnp.where(sub == k + 1, below, done)
            for i in range(i0 if k < 6 else i0 + 1, rank // 8):
                x = rows[i]
                rows[i] = x - x[:, j : j + 1] * first - x[:, j + 1 : j + 2] * second
    for m, rows in enumerate(results):
        for i, row in enumerate(rows):
            right = row[:, rank:]
            grown = (right * right * norms[:, m * rank : (m + 1) * rank]).sum(axis=1, keepdims=True)
            worse += jnp.where(grown <= LIMIT, 0.0, 1.0)
            zero = jnp.zeros_like(right)
            pair = [right, zero] if m == 0 else [zero, right]
            out[m * rank + 8 * i : m * rank + 8 * i + 8] = jnp.concatenate(pair, axis=1)
    growth[0] = jnp.sum(worse)


def basis_kernel(scale, inverse, image_q, image_k, basis_q, basis_k):
    rank = image_q.shape[0]
    for m, (image, basis) in enumerate(((image_q, basis_q), (image_k, basis_k))):
        inv = inverse[m * rank : (m + 1) * rank, m * rank : (m + 1) * rank]
        b = jnp.dot(inv, wide(image[...]), precision=EXACT, preferred_element_type=F32)
        basis[...] = (wide(b.astype(BF16)) * scale).T.astype(BF16)


def split_kernel(group, across, *refs):
    own, got, gram, other = refs[:4]
    kept, *sent = refs[4 : 4 + group.size]
    gram_out, held = refs[4 + group.size :]
    held[...] = own[...] + wide(got[...])
    size = kept.shape[0]
    cut_into(held, group, [kept] + [x.at[:size] for x in sent])
    total = gram[...] + other[...]
    gram_out[...] = total
    three = parts_of(total)
    rank = total.shape[0]
    for x in sent[: across.size - 1]:
        for i, part in enumerate(three):
            x[size + i * rank : size + (i + 1) * rank] = part


def split(own, got, gram, other, group, across):
    rows, width = own.shape
    size, extra = rows // group.size, 3 * gram.shape[0]
    sent = [vmem((size + (extra if s < across.size else 0), width), BF16) for s in range(1, group.size)]
    out = local(
        functools.partial(split_kernel, group, across),
        [own, got, gram, other],
        [vmem((size, width), F32), *sent, vmem(gram.shape, F32)],
        [vmem((rows, width), F32)],
    )
    return out[0], out[1:-1], out[-1]


def sum_kernel(*refs):
    own, received, out = refs[0], refs[1:-1], refs[-1]
    total = own[...]
    for r in received:
        total = total + wide(r[: own.shape[0]])
    out[...] = total.astype(BF16)


def finish_kernel(group, inverse, *refs):
    blocks, (copies, held) = refs[:-2], refs[-2:]
    for s, block in enumerate(blocks):
        held[group.source(s)] = wide(block[...])
    total = held[0]
    for j in range(1, len(blocks)):
        total = total + held[j]
    new = lax.dot_general(
        total, inverse[...], (((1,), (1,)), ((), ())), precision=EXACT, preferred_element_type=F32
    ).astype(BF16)
    for s in range(copies.shape[0]):
        copies[s] = new


def refresh_kernel(core, tiles_q, tile, *refs):
    own, other, basis_q, basis_k, merged_q, merged_k, out_q, out_k, new_q, new_k, held, flat = refs
    rank, d = new_q.shape
    step = pl.program_id(0)

    @pl.when(step == 0)
    def _():
        half = held.shape[0] // 2
        held[rows_at(core.pos(), half, 16)] = own[...]
        held[rows_at(core.to(1), half, 16)] = other[...]
        for t in range(0, d, LANES):
            flat[:, t : t + LANES] = wide(held[t : t + LANES]).T.astype(BF16)
        new_q[...] = flat[:rank]
        new_k[...] = flat[rank:]

    chunk = 768 if d % 768 == 0 else d

    def update(at, merged, basis, factor, out):
        rows = rows_at(at, tile, tile)
        b = basis[rows]
        for c in range(0, d, chunk):
            approx = jnp.dot(b, factor[:, c : c + chunk], preferred_element_type=F32)
            out[:, c : c + chunk] = (wide(merged[rows, c : c + chunk]) - approx).astype(BF16)

    @pl.when(step < tiles_q)
    def _():
        update(step, merged_q, basis_q, flat.at[:rank], out_q)

    @pl.when(step >= tiles_q)
    def _():
        update(step - tiles_q, merged_k, basis_k, flat.at[rank:], out_k)


def refresh(core, padded, pieces, basis_q, basis_k, merged_q, merged_k):
    rank = basis_q.shape[1]
    rows_q, d = merged_q.shape
    rows_k = merged_k.shape[0]
    tile = 2 * LANES if rows_k % (2 * LANES) == 0 else LANES
    tiles_q, tiles_k = rows_q // tile, rows_k // tile
    ins = [*pieces, basis_q, basis_k, merged_q, merged_k]
    ins = [pltpu.with_memory_space_constraint(a, pltpu.VMEM) for a in ins]
    return pl.pallas_call(
        functools.partial(refresh_kernel, core, tiles_q, tile),
        grid=(tiles_q + tiles_k,),
        in_specs=[whole()] * len(ins),
        out_specs=[
            pl.BlockSpec((tile, d), lambda i: (jnp.minimum(i, tiles_q - 1), 0)),
            pl.BlockSpec((tile, d), lambda i: (jnp.maximum(i - tiles_q, 0), 0)),
            pl.BlockSpec((rank, d), lambda i: (0, 0)),
            pl.BlockSpec((rank, d), lambda i: (0, 0)),
        ],
        out_shape=[
            jax.ShapeDtypeStruct((rows_q, d), BF16),
            jax.ShapeDtypeStruct((rows_k, d), BF16),
            jax.ShapeDtypeStruct((rank, d), BF16),
            jax.ShapeDtypeStruct((rank, d), BF16),
        ],
        scratch_shapes=[vmem((padded, 2 * rank), BF16), vmem((2 * rank, d), BF16)],
        compiler_params=pltpu.CompilerParams(vmem_limit_bytes=24 * MIB),
        cost_estimate=pl.CostEstimate(
            flops=2 * (rows_q + rows_k) * d * 256, bytes_accessed=4 * (rows_q + rows_k) * d, transcendentals=0
        ),
    )(*ins)


def sum_over(x, axes):
    size = lax.axis_size(axes)
    rows = x.shape[0]
    parts = lax.all_to_all(x.reshape(size, rows // size, x.shape[1]), axes, 0, 0).sum(0)
    parts = jnp.broadcast_to(parts, (size,) + parts.shape)
    return lax.all_to_all(parts, axes, 0, 0).reshape(x.shape)


def in_float32(grad_query, grad_key, error_query, error_key, factor_query, factor_key):
    n_dp = lax.axis_size(("z", "y"))
    errors, news = [], []
    for grad, error, factor in (
        (grad_query, error_query, factor_query),
        (grad_key, error_key, factor_key),
    ):
        merged = (wide(grad[0, 0]) + wide(error[0, 0])).astype(BF16)
        image = jnp.dot(merged, factor[0], preferred_element_type=F32)
        image = sum_over(image, ("z", "y"))
        gram = lax.dot_general(image, image, (((0,), (0,)), ((), ())), precision=EXACT)
        lower = jnp.linalg.cholesky(sum_over(gram, ("x", "core")))
        basis = jax.scipy.linalg.solve_triangular(lower, image.T, lower=True).astype(BF16)
        new = lax.dot_general(merged, basis, (((0,), (1,)), ((), ())), preferred_element_type=F32)
        new = sum_over(new, AXES).astype(BF16)
        approx = lax.dot_general(basis, new, (((0,), (1,)), ((), ())), preferred_element_type=F32)
        errors.append((wide(merged) - approx / n_dp).astype(BF16))
        news.append(new.T)
    return (*errors, *news)


def body(grad_query, grad_key, error_query, error_key, factor_query, factor_key):
    n_z, n_y, n_x, n_core = (lax.axis_size(a) for a in AXES)
    n_dp, count = n_z * n_y, n_z * n_y * n_x * n_core
    core = Group([(1, n_core)], count)
    across = Group([(n_core, n_x)], count)
    plane = Group([(n_core, n_x), (n_core * n_x, n_y)], count)
    column = Group([(n_core * n_x, n_y)], count)
    line = Group([(n_core * n_x * n_y, n_z)], count)
    rows_q, d = grad_query.shape[2:]
    rows_k = grad_key.shape[2]
    rank = factor_query.shape[2]
    unit = 16 * count
    padded = -(-d // unit) * unit
    half = padded // 2

    flat = -(-((rows_q + rows_k) // LANES * rank) // (16 * n_z)) * 16 * n_z
    merged_q, merged_k, kept, *sent = images(
        line,
        flat,
        [grad_query[0, 0], grad_key[0, 0]],
        [error_query[0, 0], error_key[0, 0]],
        [factor_query[0].T, factor_key[0].T],
    )
    shape = kept.shape
    block = local(sum_kernel, [kept, *line.scatter(sent)], [vmem(shape, BF16)])[0]
    block = local(
        functools.partial(ordered_kernel, column),
        [block, *column.gather(block)],
        [vmem(shape, BF16)],
        [vmem((n_y,) + shape, F32)],
    )[0]
    image_q, image_k, gram = local(
        functools.partial(assemble_kernel, line, rank, (rows_q, rows_k)),
        [block, *line.gather(block)],
        [vmem((rank, rows_q), BF16), vmem((rank, rows_k), BF16), vmem((rank, 2 * rank), F32)],
        [vmem((flat, LANES), BF16)],
    )

    gram_pair = core.send(gram, 1)
    operands = (image_q, image_k, merged_q, merged_k)
    got = core.send(project(core, True, half, *operands), 1)
    kept = project(core, False, half, *operands)
    kept, sent, gram = split(kept, got, gram, gram_pair, plane, across)
    received = plane.scatter(sent)
    block = local(sum_kernel, [kept, *received], [vmem(kept.shape, BF16)])[0]
    blocks = [block, *line.gather(block)]
    inverse, growth = local(
        functools.partial(inverse_kernel, across),
        [gram, *received[: n_x - 1]],
        [vmem((2 * rank, 2 * rank), F32), pltpu.SMEM((1,), F32)],
        [vmem((n_x, rank, 2 * rank), F32)],
        flops=1 << 32,
        after=[block],
    )
    basis_q, basis_k = local(
        functools.partial(basis_kernel, 1.0 / n_dp),
        [inverse, image_q, image_k],
        [vmem((rows_q, rank), BF16), vmem((rows_k, rank), BF16)],
    )

    copies = local(
        functools.partial(finish_kernel, line),
        [inverse, *blocks],
        [vmem((plane.size,) + block.shape, BF16)],
        [vmem((n_z,) + block.shape, F32)],
    )[0]

    own = lax.all_to_all(copies, ("y", "x"), 0, 0).reshape(half, 2 * rank)
    pieces = [own, core.send(own, 1)]
    results = refresh(core, padded, pieces, basis_q, basis_k, merged_q, merged_k)

    def careful(_):
        return in_float32(grad_query, grad_key, error_query, error_key, factor_query, factor_key)

    fine = growth[0] == 0.0
    error_q, error_k, new_q, new_k = lax.cond(fine, tuple, careful, results)
    return error_q[None, None], error_k[None, None], new_q.T[None], new_k.T[None]


def solution(mesh):
    n_dp, n_t = mesh.shape["dp"], mesh.shape["tensor"]
    n_z = 4 if n_dp % 4 == 0 else 1
    chips = Mesh(mesh.devices.reshape(n_z, n_dp // n_z, n_t // 2, 2), AXES)
    rows = P(("z", "y"), None, ("x", "core"), None)
    return jax.shard_map(
        body,
        mesh=chips,
        in_specs=(rows, rows, rows, rows, P(), P()),
        out_specs=(rows, rows, P(), P()),
        check_vma=False,
    )
```

```python
import functools

import jax
import jax.numpy as jnp
from jax import lax
from jax.experimental import pallas as pl
from jax.experimental.pallas import tpu as pltpu
from jax.sharding import Mesh, PartitionSpec as P

F32, BF16 = jnp.float32, jnp.bfloat16
MIB = 1 << 20
AXES = ("z", "y", "x", "core")
LIMIT = 3.0
EXACT = lax.Precision.HIGHEST
LANES = 128


def wide(a):
    return a.astype(F32)


def vmem(shape, dtype):
    return pltpu.VMEM(tuple(shape), dtype)


def whole():
    return pl.BlockSpec(memory_space=pltpu.VMEM)


def local(kernel, ins, outs, scratch=(), limit=8, flops=0, after=()):
    ins = [pltpu.with_memory_space_constraint(a, pltpu.VMEM) for a in ins]
    moved = sum(a.size * a.dtype.itemsize for a in ins)
    n_in, n_after = len(ins), len(after)

    def run(*refs):
        kernel(*refs[:n_in], *refs[n_in + n_after :])

    return pl.pallas_call(
        run,
        in_specs=[whole()] * n_in + [pl.BlockSpec(memory_space=pl.ANY)] * n_after,
        out_specs=[pl.BlockSpec(memory_space=o.memory_space) for o in outs],
        out_shape=list(outs),
        scratch_shapes=list(scratch),
        compiler_params=pltpu.CompilerParams(vmem_limit_bytes=limit * MIB),
        cost_estimate=pl.CostEstimate(flops=flops, bytes_accessed=moved, transcendentals=0),
    )(*ins, *after)


class Group:
    def __init__(self, digits, count):
        self.digits, self.count = digits, count
        self.size = 1
        for _, size in digits:
            self.size *= size
        self.pairwise = self.size & (self.size - 1) == 0

    def place(self, index):
        p, weight = 0, 1
        for stride, size in self.digits:
            p = p + (index // stride) % size * weight
            weight *= size
        return p

    def pos(self):
        p, weight = 0, 1
        index = lax.axis_index(AXES)
        for stride, size in self.digits:
            p = p + lax.rem(lax.div(index, stride), size) * weight
            weight *= size
        return p

    def to(self, step):
        if self.pairwise:
            return lax.bitwise_xor(self.pos(), step)
        return lax.rem(self.pos() + step, self.size)

    def source(self, step):
        if self.pairwise:
            return lax.bitwise_xor(self.pos(), step)
        return lax.rem(self.pos() + (self.size - step), self.size)

    def send(self, x, step):
        pairs = []
        for src in range(self.count):
            p = self.place(src)
            q = p ^ step if self.pairwise else (p + step) % self.size
            dst, weight = src, 1
            for stride, size in self.digits:
                dst += ((q // weight) % size - (p // weight) % size) * stride
                weight *= size
            pairs.append((src, dst))
        return lax.ppermute(x, AXES, pairs)

    def scatter(self, parts):
        return [self.send(x, s + 1) for s, x in enumerate(parts)]

    def gather(self, x):
        return [self.send(x, s) for s in range(1, self.size)]


def rows_at(index, size, align):
    return pl.ds(pl.multiple_of(index * size, align), size)


def blocks_at(group, size, align):
    return [rows_at(group.source(s), size, align) for s in range(group.size)]


def cut_into(held, group, outs):
    size = held.shape[0] // group.size
    for s, out in enumerate(outs):
        out[...] = held[rows_at(group.to(s), size, 8)].astype(out.dtype)


def image_kernel(group, tile, depth, *refs):
    ins, merged, outs, scratch = refs[:6], refs[6:8], refs[8 : 8 + group.size], refs[8 + group.size :]
    grads, errors, factors = ins[0:2], ins[2:4], ins[4:6]
    arrived, flat_factors, natural, held, grad_sems, error_sems, factor_sems = scratch
    rank, d = flat_factors.shape[1:]
    tiles = [(m, i) for m in (0, 1) for i in range(grads[m].shape[0] // tile)]

    def copies(n):
        m, i = tiles[n]
        rows = pl.ds(i * tile, tile)
        return (
            pltpu.make_async_copy(grads[m].at[rows], merged[m].at[rows], grad_sems.at[n]),
            pltpu.make_async_copy(errors[m].at[rows], arrived.at[n], error_sems.at[n]),
        )

    def factor_copy(m):
        return pltpu.make_async_copy(factors[m], flat_factors.at[m], factor_sems.at[m])

    def start(n):
        for c in copies(n):
            c.start()

    factor_copy(0).start()
    for n in range(min(depth, len(tiles))):
        start(n)
        if n == 0:
            factor_copy(1).start()
    for m in range(2):
        factor_copy(m).wait()
        for t in range(0, d, LANES):
            natural[m, t : t + LANES] = wide(flat_factors[m, :, t : t + LANES]).T.astype(BF16)
    chunk = 512 if d % 512 == 0 else d
    for n, (m, i) in enumerate(tiles):
        for c in copies(n):
            c.wait()
        if n + depth < len(tiles):
            start(n + depth)
        rows = pl.ds(i * tile, tile)
        image = jnp.zeros((tile, rank), F32)
        for c in range(0, d, chunk):
            cols = pl.ds(c, chunk)
            x = (wide(merged[m][rows, cols]) + wide(arrived[n, :, cols])).astype(BF16)
            merged[m][rows, cols] = x
            image += jnp.dot(x, natural[m, cols], preferred_element_type=F32)
        held[n * rank : (n + 1) * rank] = image.T
    used = len(tiles) * rank
    if used < held.shape[0]:
        held[used:] = jnp.zeros((held.shape[0] - used, held.shape[1]), F32)
    cut_into(held, group, outs)


def images(group, flat, grads, errors, factors):
    rows = [g.shape[0] for g in grads]
    d = grads[0].shape[1]
    rank = factors[0].shape[0]
    tile = LANES
    count = sum(rows) // tile
    ins = [pltpu.with_memory_space_constraint(a, pltpu.HBM) for a in (*grads, *errors, *factors)]
    cut = (flat // group.size, LANES)
    outs = [vmem((r, d), BF16) for r in rows] + [vmem(cut, F32)] + [vmem(cut, BF16)] * (group.size - 1)
    return pl.pallas_call(
        functools.partial(image_kernel, group, tile, 4),
        in_specs=[pl.BlockSpec(memory_space=pltpu.HBM)] * len(ins),
        out_specs=[whole()] * len(outs),
        out_shape=outs,
        scratch_shapes=[
            vmem((count, tile, d), BF16),
            vmem((2, rank, d), BF16),
            vmem((2, d, rank), BF16),
            vmem((flat, LANES), F32),
            pltpu.SemaphoreType.DMA((count,)),
            pltpu.SemaphoreType.DMA((count,)),
            pltpu.SemaphoreType.DMA((2,)),
        ],
        compiler_params=pltpu.CompilerParams(vmem_limit_bytes=24 * MIB),
        cost_estimate=pl.CostEstimate(
            flops=2 * sum(rows) * d * 256, bytes_accessed=4 * sum(rows) * d, transcendentals=0
        ),
    )(*ins)


def ordered_kernel(group, *refs):
    blocks, (out, held) = refs[:-2], refs[-2:]
    for s, block in enumerate(blocks):
        held[group.source(s)] = wide(block[...])
    total = held[0]
    for j in range(1, len(blocks)):
        total = total + held[j]
    out[...] = total.astype(BF16)


def assemble_kernel(group, rank, rows, *refs):
    blocks, (image_q, image_k, gram, flat) = refs[: group.size], refs[group.size :]
    for s, block in enumerate(blocks):
        size = block.shape[0]
        flat[rows_at(group.source(s), size, 16)] = block[...]
    n = 0
    for m, image_out in enumerate((image_q, image_k)):
        count = rows[m] // LANES
        parts = [flat[(n + i) * rank : (n + i + 1) * rank] for i in range(count)]
        image = jnp.concatenate(parts, axis=1) if count > 1 else parts[0]
        n += count
        image_out[...] = image
        gram[:, m * rank : (m + 1) * rank] = lax.dot_general(
            image, image, (((1,), (1,)), ((), ())), preferred_element_type=F32
        )


def project_kernel(core, other, tile, image_q, image_k, merged_q, merged_k, out):
    d = merged_q.shape[1]
    half = out.shape[0]
    first = (core.to(1) if other else core.pos()) * half
    for t in range(0, half, tile):
        start = pl.multiple_of(first + t, LANES)

        def fill(start=start, t=t):
            both = [
                jnp.dot(image[...], merged[:, pl.ds(start, tile)], preferred_element_type=F32)
                for image, merged in ((image_q, merged_q), (image_k, merged_k))
            ]
            out[t : t + tile] = jnp.concatenate(both, axis=0).T.astype(out.dtype)

        if 2 * half == d:
            fill()
        else:
            pl.when(start < d)(fill)

            @pl.when(start >= d)
            def _(t=t):
                out[t : t + tile] = jnp.zeros((tile, out.shape[1]), out.dtype)


def project(core, other, half, image_q, image_k, merged_q, merged_k):
    d = merged_q.shape[1]
    tile = next(t for t in (768, 512, 256, 128) if half % t == 0 and d % t == 0)
    return local(
        functools.partial(project_kernel, core, other, tile),
        [image_q, image_k, merged_q, merged_k],
        [vmem((half, 2 * image_q.shape[0]), BF16 if other else F32)],
        limit=16,
        flops=(merged_q.shape[0] + merged_k.shape[0]) * half * 512,
    )[0]


def parts_of(x):
    high = x.astype(BF16)
    rest = x - wide(high)
    middle = rest.astype(BF16)
    return high, middle, (rest - wide(middle)).astype(BF16)


def inverse_kernel(group, own, *refs):
    received, (out, growth, held) = refs[:-3], refs[-3:]
    rank = out.shape[0] // 2
    tail = slice(received[0].shape[0] - 3 * rank, None)
    for s, three in enumerate([parts_of(own[...])] + [r[tail] for r in received]):
        if s:
            three = [three[i * rank : (i + 1) * rank] for i in range(3)]
        high, middle, low = (wide(p) for p in three)
        held[group.source(s)] = high + (middle + low)
    lane = lax.broadcasted_iota(jnp.int32, (8, 2 * rank), 1)
    sub = lax.broadcasted_iota(jnp.int32, (8, 2 * rank), 0)
    both = held[0]
    for j in range(1, group.size):
        both += held[j]
    systems = []
    for m in range(2):
        gram = both[:, m * rank : (m + 1) * rank]
        gram = jnp.concatenate([gram, jnp.zeros((rank, rank), F32)], axis=1)
        systems.append(
            [
                jnp.where(lane == sub + (rank + 8 * i), 1.0, gram[8 * i : 8 * i + 8])
                for i in range(rank // 8)
            ]
        )
    shape = (8, 2 * rank)
    square = lax.broadcasted_iota(jnp.int32, both.shape, 0) - lax.broadcasted_iota(jnp.int32, both.shape, 1)
    norms = jnp.where((square == 0) | (square == -rank), both, 0.0).sum(axis=0, keepdims=True)
    worse = jnp.zeros((8, 1), F32)
    results = [[None] * (rank // 8) for _ in systems]
    for j in range(0, rank, 2):
        i0, k = divmod(j, 8)
        for m, rows in enumerate(systems):
            one = jnp.broadcast_to(rows[i0][k : k + 1, :], shape)
            two = jnp.broadcast_to(rows[i0][k + 1 : k + 2, :], shape)
            a = jnp.broadcast_to(one[:, j : j + 1], shape)
            b = jnp.broadcast_to(one[:, j + 1 : j + 2], shape)
            c = jnp.broadcast_to(two[:, j + 1 : j + 2], shape)
            det = 1.0 / (a * c - b * b)
            first, second = (c * one - b * two) * det, (a * two - b * one) * det
            ratio = b / a
            done = results[m][i0] if k else jnp.zeros(shape, F32)
            done = jnp.where(sub == k, one / jnp.sqrt(a), done)
            below = (two - ratio * one) / jnp.sqrt(c - ratio * b)
            results[m][i0] = jnp.where(sub == k + 1, below, done)
            for i in range(i0 if k < 6 else i0 + 1, rank // 8):
                x = rows[i]
                rows[i] = x - x[:, j : j + 1] * first - x[:, j + 1 : j + 2] * second
    for m, rows in enumerate(results):
        for i, row in enumerate(rows):
            right = row[:, rank:]
            grown = (right * right * norms[:, m * rank : (m + 1) * rank]).sum(axis=1, keepdims=True)
            worse += jnp.where(grown <= LIMIT, 0.0, 1.0)
            zero = jnp.zeros_like(right)
            pair = [right, zero] if m == 0 else [zero, right]
            out[m * rank + 8 * i : m * rank + 8 * i + 8] = jnp.concatenate(pair, axis=1)
    growth[0] = jnp.sum(worse)


def basis_kernel(scale, inverse, image_q, image_k, basis_q, basis_k):
    rank = image_q.shape[0]
    for m, (image, basis) in enumerate(((image_q, basis_q), (image_k, basis_k))):
        inv = inverse[m * rank : (m + 1) * rank, m * rank : (m + 1) * rank]
        b = jnp.dot(inv, wide(image[...]), precision=EXACT, preferred_element_type=F32)
        basis[...] = (wide(b.astype(BF16)) * scale).T.astype(BF16)


def split_kernel(group, across, *refs):
    own, got, gram, other = refs[:4]
    kept, *sent = refs[4 : 4 + group.size]
    gram_out, held = refs[4 + group.size :]
    held[...] = own[...] + wide(got[...])
    size = kept.shape[0]
    cut_into(held, group, [kept] + [x.at[:size] for x in sent])
    total = gram[...] + other[...]
    gram_out[...] = total
    three = parts_of(total)
    rank = total.shape[0]
    for x in sent[: across.size - 1]:
        for i, part in enumerate(three):
            x[size + i * rank : size + (i + 1) * rank] = part


def split(own, got, gram, other, group, across):
    rows, width = own.shape
    size, extra = rows // group.size, 3 * gram.shape[0]
    sent = [vmem((size + (extra if s < across.size else 0), width), BF16) for s in range(1, group.size)]
    out = local(
        functools.partial(split_kernel, group, across),
        [own, got, gram, other],
        [vmem((size, width), F32), *sent, vmem(gram.shape, F32)],
        [vmem((rows, width), F32)],
    )
    return out[0], out[1:-1], out[-1]


def sum_kernel(*refs):
    own, received, out = refs[0], refs[1:-1], refs[-1]
    total = own[...]
    for r in received:
        total = total + wide(r[: own.shape[0]])
    out[...] = total.astype(BF16)


def finish_kernel(group, inverse, *refs):
    blocks, (out, held) = refs[:-2], refs[-2:]
    for s, block in enumerate(blocks):
        held[group.source(s)] = wide(block[...])
    total = held[0]
    for j in range(1, len(blocks)):
        total = total + held[j]
    out[...] = lax.dot_general(
        total, inverse[...], (((1,), (1,)), ((), ())), precision=EXACT, preferred_element_type=F32
    ).astype(BF16)


def refresh_kernel(core, plane, tiles_q, tile, *refs):
    pieces, refs = refs[: 2 * plane.size], refs[2 * plane.size :]
    basis_q, basis_k, merged_q, merged_k, out_q, out_k, new_q, new_k, held, flat = refs
    rank, d = new_q.shape
    step = pl.program_id(0)

    @pl.when(step == 0)
    def _():
        half = held.shape[0] // 2
        size = half // plane.size
        for i, piece in enumerate(pieces):
            first = core.to(i // plane.size) * half + plane.source(i % plane.size) * size
            held[pl.ds(pl.multiple_of(first, 16), size)] = piece[...]
        for t in range(0, d, LANES):
            flat[:, t : t + LANES] = wide(held[t : t + LANES]).T.astype(BF16)
        new_q[...] = flat[:rank]
        new_k[...] = flat[rank:]

    chunk = 768 if d % 768 == 0 else d

    def update(at, merged, basis, factor, out):
        rows = rows_at(at, tile, tile)
        b = basis[rows]
        for c in range(0, d, chunk):
            approx = jnp.dot(b, factor[:, c : c + chunk], preferred_element_type=F32)
            out[:, c : c + chunk] = (wide(merged[rows, c : c + chunk]) - approx).astype(BF16)

    @pl.when(step < tiles_q)
    def _():
        update(step, merged_q, basis_q, flat.at[:rank], out_q)

    @pl.when(step >= tiles_q)
    def _():
        update(step - tiles_q, merged_k, basis_k, flat.at[rank:], out_k)


def refresh(core, plane, padded, pieces, basis_q, basis_k, merged_q, merged_k):
    rank = basis_q.shape[1]
    rows_q, d = merged_q.shape
    rows_k = merged_k.shape[0]
    tile = 2 * LANES if rows_k % (2 * LANES) == 0 else LANES
    tiles_q, tiles_k = rows_q // tile, rows_k // tile
    ins = [*pieces, basis_q, basis_k, merged_q, merged_k]
    ins = [pltpu.with_memory_space_constraint(a, pltpu.VMEM) for a in ins]
    return pl.pallas_call(
        functools.partial(refresh_kernel, core, plane, tiles_q, tile),
        grid=(tiles_q + tiles_k,),
        in_specs=[whole()] * len(ins),
        out_specs=[
            pl.BlockSpec((tile, d), lambda i: (jnp.minimum(i, tiles_q - 1), 0)),
            pl.BlockSpec((tile, d), lambda i: (jnp.maximum(i - tiles_q, 0), 0)),
            pl.BlockSpec((rank, d), lambda i: (0, 0)),
            pl.BlockSpec((rank, d), lambda i: (0, 0)),
        ],
        out_shape=[
            jax.ShapeDtypeStruct((rows_q, d), BF16),
            jax.ShapeDtypeStruct((rows_k, d), BF16),
            jax.ShapeDtypeStruct((rank, d), BF16),
            jax.ShapeDtypeStruct((rank, d), BF16),
        ],
        scratch_shapes=[vmem((padded, 2 * rank), BF16), vmem((2 * rank, d), BF16)],
        compiler_params=pltpu.CompilerParams(vmem_limit_bytes=24 * MIB),
        cost_estimate=pl.CostEstimate(
            flops=2 * (rows_q + rows_k) * d * 256, bytes_accessed=4 * (rows_q + rows_k) * d, transcendentals=0
        ),
    )(*ins)


def sum_over(x, axes):
    size = lax.axis_size(axes)
    rows = x.shape[0]
    parts = lax.all_to_all(x.reshape(size, rows // size, x.shape[1]), axes, 0, 0).sum(0)
    parts = jnp.broadcast_to(parts, (size,) + parts.shape)
    return lax.all_to_all(parts, axes, 0, 0).reshape(x.shape)


def in_float32(grad_query, grad_key, error_query, error_key, factor_query, factor_key):
    n_dp = lax.axis_size(("z", "y"))
    errors, news = [], []
    for grad, error, factor in (
        (grad_query, error_query, factor_query),
        (grad_key, error_key, factor_key),
    ):
        merged = (wide(grad[0, 0]) + wide(error[0, 0])).astype(BF16)
        image = jnp.dot(merged, factor[0], preferred_element_type=F32)
        image = sum_over(image, ("z", "y"))
        gram = lax.dot_general(image, image, (((0,), (0,)), ((), ())), precision=EXACT)
        lower = jnp.linalg.cholesky(sum_over(gram, ("x", "core")))
        basis = jax.scipy.linalg.solve_triangular(lower, image.T, lower=True).astype(BF16)
        new = lax.dot_general(merged, basis, (((0,), (1,)), ((), ())), preferred_element_type=F32)
        new = sum_over(new, AXES).astype(BF16)
        approx = lax.dot_general(basis, new, (((0,), (1,)), ((), ())), preferred_element_type=F32)
        errors.append((wide(merged) - approx / n_dp).astype(BF16))
        news.append(new.T)
    return (*errors, *news)


def body(grad_query, grad_key, error_query, error_key, factor_query, factor_key):
    n_z, n_y, n_x, n_core = (lax.axis_size(a) for a in AXES)
    n_dp, count = n_z * n_y, n_z * n_y * n_x * n_core
    core = Group([(1, n_core)], count)
    across = Group([(n_core, n_x)], count)
    plane = Group([(n_core, n_x), (n_core * n_x, n_y)], count)
    column = Group([(n_core * n_x, n_y)], count)
    line = Group([(n_core * n_x * n_y, n_z)], count)
    rows_q, d = grad_query.shape[2:]
    rows_k = grad_key.shape[2]
    rank = factor_query.shape[2]
    unit = 16 * count
    padded = -(-d // unit) * unit
    half = padded // 2

    flat = -(-((rows_q + rows_k) // LANES * rank) // (16 * n_z)) * 16 * n_z
    merged_q, merged_k, kept, *sent = images(
        line,
        flat,
        [grad_query[0, 0], grad_key[0, 0]],
        [error_query[0, 0], error_key[0, 0]],
        [factor_query[0].T, factor_key[0].T],
    )
    shape = kept.shape
    block = local(sum_kernel, [kept, *line.scatter(sent)], [vmem(shape, BF16)])[0]
    block = local(
        functools.partial(ordered_kernel, column),
        [block, *column.gather(block)],
        [vmem(shape, BF16)],
        [vmem((n_y,) + shape, F32)],
    )[0]
    image_q, image_k, gram = local(
        functools.partial(assemble_kernel, line, rank, (rows_q, rows_k)),
        [block, *line.gather(block)],
        [vmem((rank, rows_q), BF16), vmem((rank, rows_k), BF16), vmem((rank, 2 * rank), F32)],
        [vmem((flat, LANES), BF16)],
    )

    gram_pair = core.send(gram, 1)
    operands = (image_q, image_k, merged_q, merged_k)
    got = core.send(project(core, True, half, *operands), 1)
    kept = project(core, False, half, *operands)
    kept, sent, gram = split(kept, got, gram, gram_pair, plane, across)
    received = plane.scatter(sent)
    block = local(sum_kernel, [kept, *received], [vmem(kept.shape, BF16)])[0]
    blocks = [block, *line.gather(block)]
    inverse, growth = local(
        functools.partial(inverse_kernel, across),
        [gram, *received[: n_x - 1]],
        [vmem((2 * rank, 2 * rank), F32), pltpu.SMEM((1,), F32)],
        [vmem((n_x, rank, 2 * rank), F32)],
        flops=1 << 32,
        after=[block],
    )
    basis_q, basis_k = local(
        functools.partial(basis_kernel, 1.0 / n_dp),
        [inverse, image_q, image_k],
        [vmem((rows_q, rank), BF16), vmem((rows_k, rank), BF16)],
    )

    new = local(
        functools.partial(finish_kernel, line),
        [inverse, *blocks],
        [vmem(block.shape, BF16)],
        [vmem((n_z,) + block.shape, F32)],
    )[0]

    pieces = [new, *plane.gather(new)]
    pieces += [core.send(p, 1) for p in pieces]
    results = refresh(core, plane, padded, pieces, basis_q, basis_k, merged_q, merged_k)

    def careful(_):
        return in_float32(grad_query, grad_key, error_query, error_key, factor_query, factor_key)

    fine = growth[0] == 0.0
    error_q, error_k, new_q, new_k = lax.cond(fine, tuple, careful, results)
    return error_q[None, None], error_k[None, None], new_q.T[None], new_k.T[None]


def solution(mesh):
    n_dp, n_t = mesh.shape["dp"], mesh.shape["tensor"]
    n_z = 4 if n_dp % 4 == 0 else 1
    chips = Mesh(mesh.devices.reshape(n_z, n_dp // n_z, n_t // 2, 2), AXES)
    rows = P(("z", "y"), None, ("x", "core"), None)
    return jax.shard_map(
        body,
        mesh=chips,
        in_specs=(rows, rows, rows, rows, P(), P()),
        out_specs=(rows, rows, P(), P()),
        check_vma=False,
    )
```
